32 devices in a mesh: groups: 2 (over y), region: 4 (over z), lag: 2 (over x), member: 2 (over core).
Axes of the slice: x: 2, y: 2, z: 4, core: 2. Of those that a mesh axis runs over, the one named last changes fastest.
Arguments:
- snapshots: bfloat16 [4, 64, 512, 128], P(('groups', 'lag'), 'member', 'region'), parts along dimension 0, may hold values from -6 to 6
- current: float32 [128, 512, 128], P(('groups', 'lag', 'member'), 'region'), parts along dimension 0, may hold values from -6 to 6
- diffusivity: float32 [512, 128], P('region'), may hold values from 0.02 to 0.2
- landmask: int32 [512, 128], P('region'), may hold values 0 or 1
- obs_cell: int32 [65536], P(('groups', 'region')), parts along dimension 0, may hold values from 0 to 16383
- obs_value: float32 [65536], P(('groups', 'region')), parts along dimension 0, may hold values from -6 to 6
- obs_weight: float32 [65536], P(('groups', 'region')), parts along dimension 0, may hold values from 0.25 to 4
- tile_obs: int32 [1024, 512], P(('groups', 'region')), parts along dimension 0, may hold values from 0 to 24575
- tile_count: int32 [1024], P(('groups', 'region')), parts along dimension 0, may hold values from 32 to 512, as said below
Outputs:
- smoothed: bfloat16 [4, 64, 512, 128], P(('groups', 'lag'), 'member', 'region'), parts along dimension 0
- analysis: bfloat16 [128, 512, 128], P(('groups', 'lag', 'member'), 'region'), parts along dimension 0
The draws below stay inside these ranges and needn't reach their ends.
There are 2 independent parts, one for each index of `groups`. The reference program is written for one: setup_inputs(seed, part) draws one part's arguments, and reference() takes and returns one part's arrays. A program takes and returns all parts, laid end to end along the dimension named above; an argument that names none is the same for every part. Nothing has to cross between parts.
Inputs may be any that keep to these rules, and one draw needn't show every extreme that they name: tile_count is skewed over tiles; some tile of every draw uses all 512 entries.
All inputs are finite; a program needn't handle non-finite values. No bound on the sum of `landmask` on one device may be relied on, other than what follows from the above.
Results may differ from the reference program's by a relative error of at most 0.012.
Values may be sent and summed in bfloat16 or wider, within the bound.
A program may use at most 128 MiB of HBM per device.

```python
import math
import jax
import jax.numpy as jnp
from jax import lax

M = 64
ROWS_DEV = 128
COLS = 128
OBS_DEV = 8192
OBS_MAX = 512
STEPS = 2
LAG = 2
ROWS = 512
OBS = 32768


def draw_tile_count(key, part):
    first, second, third = jax.random.split(jax.random.fold_in(key, 11), 3)
    level = jax.random.randint(first, (ROWS,), 0, 4)
    top_count = OBS_MAX // jnp.left_shift(jnp.ones_like(level), level)
    reduction = jax.random.randint(second, (ROWS,), 0, top_count // 2 + 1)
    counts = top_count - reduction
    chosen = jax.random.randint(third, (), 0, ROWS)
    counts = jnp.where(jnp.arange(ROWS, dtype=jnp.int32) == chosen, OBS_MAX, counts)
    return counts.astype(jnp.int32)


def place_ends(entries, own_key, smallest, top_value):
    shape = entries.shape
    spot = [jax.random.randint(jax.random.fold_in(own_key, axis), (), 0, shape[axis]) for axis in range(len(shape))]
    entries = entries.at[tuple(spot)].set(smallest)
    longest = shape.index(max(shape))
    spot[longest] = (spot[longest] + 1) % shape[longest]
    return entries.at[tuple(spot)].set(top_value)


def levels(rng, shape, pieces, smallest, top_value):
    factor_of, own = 1.0, jax.random.fold_in(rng, 6)
    for axis_at, shards_of in pieces:
        heights = jnp.exp(jax.random.uniform(jax.random.fold_in(own, axis_at), (shards_of,), jnp.float32, smallest / len(pieces), top_value / len(pieces)))
        factor_of = factor_of * jnp.repeat(heights, shape[axis_at] // shards_of).reshape([-1 if axis == axis_at else 1 for axis in range(len(shape))])
    return factor_of


def normal_values(own_key, extent, scale, reach, pieces=(), kind=jnp.bfloat16):
    result = jax.random.normal(own_key, extent, jnp.float32) * scale
    if len(pieces) > 0:
        result = levels(own_key, extent, pieces, -0.22, 0.18) * result
    return jnp.clip(result, min=-reach, max=reach).astype(kind)


def setup_inputs(seed: int = 0, part: int = 0) -> dict:
    arg_keys = jax.random.split(jax.random.key(seed), 10)
    part_keys = jax.random.split(jax.random.fold_in(arg_keys[9], part), 10)
    snapshots = normal_values(part_keys[0], (LAG, M, ROWS, COLS), 1.0, 6.0, ((0, 2), (1, 2), (2, 4)))
    current = normal_values(part_keys[1], (M, ROWS, COLS), 1.0, 6.0, ((0, 4), (1, 4)), jnp.float32)
    diffusivity = jnp.clip(jnp.exp(math.log(0.2) - 2.3025851 * jax.random.uniform(arg_keys[2], (ROWS, COLS), jnp.float32) ** levels(arg_keys[2], (ROWS, COLS), ((0, 4),), -0.2, 0.2)), 0.02, 0.2)
    landmask = place_ends((jax.random.randint(arg_keys[3], (ROWS, COLS), 0, 8) < 7).astype(jnp.int32), jax.random.fold_in(arg_keys[3], 1), 0, 1)
    obs_cell = place_ends(jax.random.randint(part_keys[4], (OBS,), 0, ROWS_DEV * COLS), jax.random.fold_in(part_keys[4], 1), 0, (ROWS_DEV * COLS) - 1).astype(jnp.int32)
    obs_value = normal_values(part_keys[5], (OBS,), 1.0, 6.0, ((0, 4),), jnp.float32)
    obs_weight = jnp.clip(jnp.exp(math.log(4.0) - 2.7725887 * jax.random.uniform(part_keys[6], (OBS,), jnp.float32) ** levels(part_keys[6], (OBS,), ((0, 4),), -0.2, 0.2)), 0.25, 4.0)
    tile_obs = place_ends(jax.random.randint(part_keys[7], (ROWS, OBS_MAX), 0, 3 * OBS_DEV), jax.random.fold_in(part_keys[7], 1), 0, (3 * OBS_DEV) - 1).astype(jnp.int32)
    tile_count = draw_tile_count(jax.random.fold_in(jax.random.fold_in(arg_keys[9], part), 71), part)
    return {"snapshots": snapshots, "current": current, "diffusivity": diffusivity, "landmask": landmask, "obs_cell": obs_cell, "obs_value": obs_value, "obs_weight": obs_weight, "tile_obs": tile_obs, "tile_count": tile_count}


def relax(padded, diffusion, sea_mask):
    centre = padded[:, 1:-1]
    upper_row = padded[:, :-2]
    lower_row = padded[:, 2:]
    right_cell = jnp.roll(centre, 1, axis=2)
    left_cell = jnp.roll(centre, -1, axis=2)
    return sea_mask * (centre + diffusion * (upper_row + lower_row + right_cell + left_cell - 4.0 * centre))

def mixing_block(anomaly, innovation, obs_weight, window_index, live_mask):
    picked = jnp.take(anomaly, window_index, axis=1)
    obs_scale = jnp.take(obs_weight, window_index) * live_mask
    residual_obs = jnp.take(innovation, window_index)
    weighted = picked * obs_scale[None]
    members = anomaly.shape[0]
    precision_matrix = jnp.einsum('mbk,nbk->bmn', weighted, picked, precision=lax.Precision.HIGHEST) + (members - 1.0) * jnp.eye(members, dtype=jnp.float32)
    mean_rhs = jnp.einsum('mbk,bk->bm', weighted, residual_obs, precision=lax.Precision.HIGHEST)
    factor = jnp.linalg.cholesky(precision_matrix)
    partial_solve = jax.scipy.linalg.solve_triangular(factor, mean_rhs[:, :, None], lower=True)
    mean_weight = jax.scipy.linalg.solve_triangular(factor, partial_solve, lower=True, trans=1)[:, :, 0]
    identity = jnp.broadcast_to(jnp.eye(members, dtype=jnp.float32), precision_matrix.shape)
    spread = jnp.sqrt(members - 1.0) * jax.scipy.linalg.solve_triangular(factor, identity, lower=True, trans=1)
    weights = spread + mean_weight[:, :, None]
    mixing = weights + (1.0 - lax.optimization_barrier(jnp.sum(weights, axis=1, keepdims=True))) / members
    return mixing.astype(jnp.bfloat16)

def tile_mixing(anomaly, innovation, obs_weight, window_index, live_mask):
    block_count = window_index.shape[0] // 8

    def one_block(packed):
        return mixing_block(anomaly, innovation, obs_weight, packed[0], packed[1])
    mixed = lax.map(one_block, (window_index.reshape(block_count, 8, -1), live_mask.reshape(block_count, 8, -1)))
    return mixed.reshape(-1, mixed.shape[2], mixed.shape[3])

def reference(snapshots, current, diffusivity, landmask, obs_cell, obs_value, obs_weight, tile_obs, tile_count):
    sea_mask = landmask.astype(jnp.float32)
    field_now = current
    for substep in range(STEPS):
        padded = jnp.pad(field_now, ((0, 0), (1, 1), (0, 0)))
        field_now = relax(padded, diffusivity, sea_mask)
    newest = field_now.astype(jnp.bfloat16)
    flat_field = newest.reshape(M, ROWS * COLS)
    cell_index = jnp.arange(OBS, dtype=jnp.int32) // OBS_DEV * (ROWS_DEV * COLS) + obs_cell
    observed = jnp.take(flat_field, cell_index, axis=1).astype(jnp.float32)
    obs_mean = lax.optimization_barrier(jnp.mean(observed, axis=0))
    anomaly = jnp.pad(observed - obs_mean, ((0, 0), (OBS_DEV, OBS_DEV)))
    innovation = jnp.pad(obs_value - obs_mean, (OBS_DEV, OBS_DEV))
    weight_wide = jnp.pad(obs_weight, (OBS_DEV, OBS_DEV))
    window_index = (jnp.arange(ROWS, dtype=jnp.int32) // ROWS_DEV)[:, None] * OBS_DEV + tile_obs
    live_mask = (jnp.arange(OBS_MAX, dtype=jnp.int32)[None, :] < tile_count[:, None]).astype(jnp.float32)
    mixing = tile_mixing(anomaly, innovation, weight_wide, window_index, live_mask)
    mixing_wide = mixing.astype(jnp.float32)
    smoothed = jnp.einsum('lmtc,tmn->lntc', snapshots.astype(jnp.float32), mixing_wide).astype(jnp.bfloat16)
    analysis = jnp.einsum('mtc,tmn->ntc', newest.astype(jnp.float32), mixing_wide).astype(jnp.bfloat16)
    return (smoothed, analysis)
```

```python
import functools

import jax
import jax.numpy as jnp
from jax import lax
from jax.experimental import pallas as pl
from jax.experimental.pallas import tpu as pltpu
from jax.sharding import PartitionSpec as P

STEPS = 2
LANES = 128
VMEM_BYTES = 56 * 1024 * 1024


def with_halo(array, sides, width):
    for axis, dim in sides:
        size, length = (lax.axis_size(axis), array.shape[dim])
        up = [(i, (i + 1) % size) for i in range(size - 1)]
        down = [(j, i) for i, j in up]
        last = lax.slice_in_dim(array, length - width, length, axis=dim)
        leading = lax.slice_in_dim(array, 0, width, axis=dim)
        before = lax.ppermute(last, axis, up)
        after = lax.ppermute(leading, axis, down)
        array = jnp.concatenate([before, array, after], axis=dim)
    return array


def relax(padded, diffusion, sea_mask):
    centre = padded[:, 1:-1]
    upper_row = padded[:, :-2]
    lower_row = padded[:, 2:]
    right_cell = jnp.roll(centre, 1, axis=2)
    left_cell = jnp.roll(centre, -1, axis=2)
    return sea_mask * (
        centre + diffusion * (upper_row + lower_row + right_cell + left_cell - 4.0 * centre)
    )


NT = (((1,), (1,)), ((), ()))
TN = (((0,), (0,)), ((), ()))


def identity():
    row = lax.broadcasted_iota(jnp.int32, (LANES, LANES), 0)
    col = lax.broadcasted_iota(jnp.int32, (LANES, LANES), 1)
    return (row == col).astype(jnp.bfloat16)


def vmem_call(kernel, out_shape, scratch_shapes, in_spaces, flops):
    return pl.pallas_call(
        kernel,
        out_shape=out_shape,
        in_specs=[pl.BlockSpec(memory_space=space) for space in in_spaces],
        out_specs=jax.tree.map(lambda _: pl.BlockSpec(memory_space=pltpu.VMEM), out_shape),
        scratch_shapes=scratch_shapes,
        compiler_params=pltpu.CompilerParams(vmem_limit_bytes=VMEM_BYTES),
        cost_estimate=pl.CostEstimate(flops=flops, bytes_accessed=1 << 22, transcendentals=0),
    )


def sample_kernel(cell_ref, field_ref, out_ref, table, picked):
    owners, rows, own, cols = field_ref.shape
    members = owners * own
    eye = identity()

    def build(r, carry):
        part = field_ref[:, r].reshape(members, cols)
        table[pl.ds(pl.multiple_of(r * cols, cols), cols), :members] = lax.dot_general(
            eye, part, NT, preferred_element_type=jnp.float32
        )
        return carry

    lax.fori_loop(0, rows, build, 0, unroll=4)
    picked[:, members:] = jnp.zeros((LANES, LANES - members), jnp.float32)

    def block(b, carry):
        base = pl.multiple_of(b * LANES, LANES)

        def rows16(g, inner):
            for q in range(16):
                k = g * 16 + q
                picked[pl.ds(k, 1), :members] = table[pl.ds(cell_ref[base + k], 1), :members]
            return inner

        lax.fori_loop(0, LANES // 16, rows16, 0, unroll=True)
        flipped = picked[...].T
        out_ref[:, pl.ds(base, LANES)] = flipped[:members].astype(jnp.bfloat16)
        return carry

    lax.fori_loop(0, cell_ref.shape[0] // LANES, block, 0)


def mixing_kernel(
    count_ref, index_ref, before_ref, own_ref, after_ref, info_ref, out_ref,
    table, picked, gram, chol, inv, wide,
):
    share = count_ref.shape[0]
    entries = index_ref.shape[0] // share
    members, obs = own_ref.shape
    blocks = obs // LANES
    eye = identity()

    for part, ref in enumerate((before_ref, own_ref, after_ref)):

        def build(b, carry, part=part, ref=ref):
            sample = ref[:, pl.ds(pl.multiple_of(b * LANES, LANES), LANES)].astype(jnp.float32)
            mean = jnp.sum(sample, axis=0, keepdims=True) * (1.0 / members)
            value = info_ref[0, pl.ds(part * blocks + b, 1), :]
            weight = info_ref[1, pl.ds(part * blocks + b, 1), :]
            row = lax.broadcasted_iota(jnp.int32, (LANES - members, LANES), 0)
            extra = jnp.where(row == 0, value - mean, jnp.where(row == 1, weight, 0.0))
            rows = jnp.concatenate([sample - mean, extra], axis=0).astype(jnp.bfloat16)
            table[pl.ds(pl.multiple_of((part * blocks + b) * LANES, LANES), LANES), :] = (
                lax.dot_general(eye, rows, NT, preferred_element_type=jnp.float32)
            )
            return carry

        lax.fori_loop(0, blocks, build, 0, unroll=4)

    def tile(t, carry):
        count = count_ref[t]
        first = t * entries

        def rows16(g, inner):
            for q in range(16):
                k = g * 16 + q
                picked[pl.ds(k, 1), :] = table[pl.ds(index_ref[first + k], 1), :]
            return inner

        lax.fori_loop(0, (count + 15) // 16, rows16, 0)

        def chunk(c, total):
            base = pl.multiple_of(c * LANES, LANES)
            rows = picked[pl.ds(base, LANES), :]
            live = lax.broadcasted_iota(jnp.int32, (LANES, LANES), 0) + base < count
            rows = jnp.where(live, rows, 0.0)
            scaled = (rows * rows[:, members + 1 : members + 2]).astype(jnp.bfloat16)
            return total + lax.dot_general(
                rows.astype(jnp.bfloat16), scaled, TN, preferred_element_type=jnp.float32
            )

        gram[t] = lax.fori_loop(
            0, (count + LANES - 1) // LANES, chunk, jnp.zeros((LANES, LANES), jnp.float32)
        )
        return carry

    lax.fori_loop(0, share, tile, 0)

    copies = LANES // share

    def in_lanes(m):
        return jnp.concatenate([gram[:, m, :]] * copies, axis=0).T[:members]

    row_id = lax.broadcasted_iota(jnp.int32, (members, LANES), 0)
    for m in range(members):
        chol[m] = in_lanes(m) + jnp.where(row_id == m, members - 1.0, 0.0)
    rhs = in_lanes(members)

    width = 4
    for p in range(members // width):
        low = p * width // 8 * 8
        columns = [chol[p * width + q, low:, :] for q in range(width)]

        def eliminate(j, cols, p=p, low=low):
            left = chol[j, low:, :]
            return tuple(
                cols[q] - left * left[p * width + q - low : p * width + q - low + 1]
                for q in range(width)
            )

        columns = list(lax.fori_loop(0, p * width, eliminate, tuple(columns)))
        for q in range(width):
            at = p * width + q - low
            columns[q] = columns[q] * lax.rsqrt(columns[q][at : at + 1])
            for later in range(q + 1, width):
                spot = p * width + later - low
                columns[later] = columns[later] - columns[q] * columns[q][spot : spot + 1]
            chol[p * width + q, low:, :] = columns[q]

    for p in range(members // width):
        high = (p * width // 8 + 1) * 8
        ids = row_id[:high]
        rows = [jnp.where(ids == p * width + q, 1.0, 0.0) for q in range(width)]

        def substitute(j, rows, p=p, high=high):
            solved = inv[j, :high, :]
            group = chol[j, pl.ds(p * width // 8 * 8, 8), :]
            at = p * width % 8
            return tuple(
                rows[q] - solved * group[at + q : at + q + 1] for q in range(width)
            )

        rows = list(lax.fori_loop(0, p * width, substitute, tuple(rows)))
        for q in range(width):
            n = p * width + q
            rows[q] = rows[q] / chol[n, n : n + 1, :]
            for later in range(q + 1, width):
                spot = p * width + later
                rows[later] = rows[later] - rows[q] * chol[n, spot : spot + 1, :]
            inv[n, :high, :] = rows[q]
            if high < members:
                inv[n, high:, :] = jnp.zeros((members - high, LANES), jnp.float32)

    def apply(n, mean_weight):
        solved = inv[n]
        return mean_weight + solved * jnp.sum(solved * rhs, axis=0, keepdims=True)

    mean_weight = lax.fori_loop(0, members, apply, jnp.zeros((members, LANES), jnp.float32))
    root = float(members - 1) ** 0.5
    for n in range(members):
        weights = root * inv[n] + mean_weight
        mixed = weights + (1.0 - jnp.sum(weights, axis=0, keepdims=True)) * (1.0 / members)
        wide[:, n, :] = mixed.T[:share]
    out_ref[...] = wide[...].astype(jnp.bfloat16)


def update_kernel(snap_ref, snap_mix_ref, field_ref, field_mix_ref, smooth_ref, analysis_ref):
    owners, tiles, own, cols = field_ref.shape

    def tile(t, carry):
        smooth_ref[t] = jnp.dot(
            snap_mix_ref[t],
            snap_ref[:, t].reshape(owners * own, cols),
            preferred_element_type=jnp.float32,
        ).astype(jnp.bfloat16)
        analysis_ref[t] = jnp.dot(
            field_mix_ref[t],
            field_ref[:, t].reshape(owners * own, cols),
            preferred_element_type=jnp.float32,
        ).astype(jnp.bfloat16)
        return carry

    lax.fori_loop(0, tiles, tile, 0, unroll=4)


def halo_parts(array, axis, dim, width):
    size, length = lax.axis_size(axis), array.shape[dim]
    up = [(i, (i + 1) % size) for i in range(size - 1)]
    down = [(j, i) for i, j in up]
    before = lax.ppermute(lax.slice_in_dim(array, length - width, length, axis=dim), axis, up)
    after = lax.ppermute(lax.slice_in_dim(array, 0, width, axis=dim), axis, down)
    return before, after


def local(
    snapshots, current, diffusivity, landmask, obs_cell, obs_value, obs_weight, tile_obs, tile_count
):
    sea_mask = landmask.astype(jnp.float32)
    field_now = current
    for substep in range(STEPS):
        padded = with_halo(field_now, (("region", 1),), 1)
        field_now = relax(padded, diffusivity, sea_mask)
    newest = field_now.astype(jnp.bfloat16)
    own_members = newest.shape[0]
    obs_count = obs_cell.shape[0]
    obs_info = jnp.stack([obs_value, obs_weight])
    window_info = with_halo(obs_info.astype(jnp.bfloat16), (("region", 1),), obs_count).astype(
        obs_info.dtype
    )
    group_size = lax.axis_size(("lag", "member"))
    group_rank = lax.axis_index(("lag", "member"))
    by_row = newest.transpose(1, 0, 2)
    everyone = lax.all_gather(by_row, ("lag", "member"), axis=0)
    members = group_size * own_members
    vmem, smem = pltpu.VMEM, pltpu.SMEM
    rows, cols = newest.shape[1:]
    sampled = vmem_call(
        sample_kernel,
        jax.ShapeDtypeStruct((members, obs_count), jnp.bfloat16),
        [pltpu.VMEM((rows * cols, LANES), jnp.float32), pltpu.VMEM((LANES, LANES), jnp.float32)],
        (smem, vmem),
        10**8,
    )(obs_cell, everyone)
    before, after = halo_parts(sampled, "region", 1, obs_count)
    share = tile_obs.shape[0] // group_size
    first_tile = group_rank * share
    my_index = lax.dynamic_slice_in_dim(tile_obs, first_tile, share, 0).reshape(-1)
    my_count = lax.dynamic_slice_in_dim(tile_count, first_tile, share, 0)
    mine = vmem_call(
        mixing_kernel,
        jax.ShapeDtypeStruct((share, members, members), jnp.bfloat16),
        [
            pltpu.VMEM((3 * obs_count, LANES), jnp.float32),
            pltpu.VMEM((tile_obs.shape[1], LANES), jnp.float32),
            pltpu.VMEM((share, LANES, LANES), jnp.float32),
            pltpu.VMEM((members, members, LANES), jnp.float32),
            pltpu.VMEM((members, members, LANES), jnp.float32),
            pltpu.VMEM((share, members, members), jnp.float32),
        ],
        (smem, smem, vmem, vmem, vmem, vmem),
        10**9,
    )(my_count, my_index, before, sampled, after, window_info.reshape(2, -1, LANES))
    mixing = lax.all_gather(mine, ("lag", "member"), axis=0, tiled=True)
    member_rank = lax.axis_index("member")
    half_members = snapshots.shape[1]
    snap_mix = lax.dynamic_slice_in_dim(mixing, member_rank * half_members, half_members, 1)
    field_mix = lax.dynamic_slice_in_dim(mixing, group_rank * own_members, own_members, 1)
    snaps = lax.all_gather(snapshots[0].transpose(1, 0, 2), "member", axis=0)
    smoothed, analysis = vmem_call(
        update_kernel,
        (
            jax.ShapeDtypeStruct((rows, half_members, cols), jnp.bfloat16),
            jax.ShapeDtypeStruct((rows, own_members, cols), jnp.bfloat16),
        ),
        [],
        (vmem,) * 4,
        10**8,
    )(snaps, snap_mix, everyone, field_mix)
    return (smoothed.transpose(1, 0, 2)[None], analysis.transpose(1, 0, 2))


def solution(mesh):
    placed = (
        P(("groups", "lag"), "member", "region", None),
        P(("groups", "lag", "member"), "region", None),
        P("region", None),
        P("region", None),
        P(("groups", "region")),
        P(("groups", "region")),
        P(("groups", "region")),
        P(("groups", "region"), None),
        P(("groups", "region")),
    )
    return jax.shard_map(
        local,
        mesh=mesh,
        in_specs=placed,
        out_specs=(
            P(("groups", "lag"), "member", "region", None),
            P(("groups", "lag", "member"), "region", None),
        ),
        check_vma=False,
    )
```

```python
import functools

import jax
import jax.numpy as jnp
from jax import lax
from jax.experimental import pallas as pl
from jax.experimental.pallas import tpu as pltpu
from jax.sharding import PartitionSpec as P

STEPS = 2
LANES = 128
VMEM_BYTES = 56 * 1024 * 1024


def with_halo(array, sides, width):
    for axis, dim in sides:
        size, length = (lax.axis_size(axis), array.shape[dim])
        up = [(i, (i + 1) % size) for i in range(size - 1)]
        down = [(j, i) for i, j in up]
        last = lax.slice_in_dim(array, length - width, length, axis=dim)
        leading = lax.slice_in_dim(array, 0, width, axis=dim)
        before = lax.ppermute(last, axis, up)
        after = lax.ppermute(leading, axis, down)
        array = jnp.concatenate([before, array, after], axis=dim)
    return array


def relax(padded, diffusion, sea_mask):
    centre = padded[:, 1:-1]
    upper_row = padded[:, :-2]
    lower_row = padded[:, 2:]
    right_cell = jnp.roll(centre, 1, axis=2)
    left_cell = jnp.roll(centre, -1, axis=2)
    return sea_mask * (
        centre + diffusion * (upper_row + lower_row + right_cell + left_cell - 4.0 * centre)
    )


NT = (((1,), (1,)), ((), ()))
TN = (((0,), (0,)), ((), ()))


def identity():
    row = lax.broadcasted_iota(jnp.int32, (LANES, LANES), 0)
    col = lax.broadcasted_iota(jnp.int32, (LANES, LANES), 1)
    return (row == col).astype(jnp.bfloat16)


def vmem_call(kernel, out_shape, scratch_shapes, in_spaces, flops):
    return pl.pallas_call(
        kernel,
        out_shape=out_shape,
        in_specs=[pl.BlockSpec(memory_space=space) for space in in_spaces],
        out_specs=jax.tree.map(lambda _: pl.BlockSpec(memory_space=pltpu.VMEM), out_shape),
        scratch_shapes=scratch_shapes,
        compiler_params=pltpu.CompilerParams(vmem_limit_bytes=VMEM_BYTES),
        cost_estimate=pl.CostEstimate(flops=flops, bytes_accessed=1 << 22, transcendentals=0),
    )


def sample_kernel(cell_ref, field_ref, out_ref, table, picked):
    owners, rows, own, cols = field_ref.shape
    members = owners * own
    eye = identity()

    def build(r, carry):
        part = field_ref[:, r].reshape(members, cols)
        table[pl.ds(pl.multiple_of(r * cols, cols), cols), :members] = lax.dot_general(
            eye, part, NT, preferred_element_type=jnp.float32
        )
        return carry

    lax.fori_loop(0, rows, build, 0, unroll=4)
    picked[:, members:] = jnp.zeros((LANES, LANES - members), jnp.float32)

    def block(b, carry):
        base = pl.multiple_of(b * LANES, LANES)

        def rows16(g, inner):
            for q in range(16):
                k = g * 16 + q
                picked[pl.ds(k, 1), :members] = table[pl.ds(cell_ref[base + k], 1), :members]
            return inner

        lax.fori_loop(0, LANES // 16, rows16, 0, unroll=True)
        flipped = picked[...].T
        out_ref[:, pl.ds(base, LANES)] = flipped[:members].astype(jnp.bfloat16)
        return carry

    lax.fori_loop(0, cell_ref.shape[0] // LANES, block, 0)


def mixing_kernel(
    count_ref, index_ref, before_ref, own_ref, after_ref, info_ref, out_ref,
    table, picked, gram, chol, inv, wide,
):
    share = count_ref.shape[0]
    entries = index_ref.shape[0] // share
    members, obs = own_ref.shape
    blocks = obs // LANES
    eye = identity()

    for part, ref in enumerate((before_ref, own_ref, after_ref)):

        def build(b, carry, part=part, ref=ref):
            sample = ref[:, pl.ds(pl.multiple_of(b * LANES, LANES), LANES)].astype(jnp.float32)
            mean = jnp.sum(sample, axis=0, keepdims=True) * (1.0 / members)
            value = info_ref[0, pl.ds(part * blocks + b, 1), :]
            weight = info_ref[1, pl.ds(part * blocks + b, 1), :]
            row = lax.broadcasted_iota(jnp.int32, (LANES - members, LANES), 0)
            extra = jnp.where(row == 0, value - mean, jnp.where(row == 1, weight, 0.0))
            rows = jnp.concatenate([sample - mean, extra], axis=0).astype(jnp.bfloat16)
            table[pl.ds(pl.multiple_of((part * blocks + b) * LANES, LANES), LANES), :] = (
                lax.dot_general(eye, rows, NT, preferred_element_type=jnp.float32)
            )
            return carry

        lax.fori_loop(0, blocks, build, 0, unroll=4)

    def tile(t, carry):
        count = count_ref[t]
        first = t * entries

        def rows16(g, inner):
            for q in range(16):
                k = g * 16 + q
                picked[pl.ds(k, 1), :] = table[pl.ds(index_ref[first + k], 1), :]
            return inner

        lax.fori_loop(0, (count + 15) // 16, rows16, 0)

        def chunk(c, total):
            base = pl.multiple_of(c * LANES, LANES)
            rows = picked[pl.ds(base, LANES), :]
            live = lax.broadcasted_iota(jnp.int32, (LANES, LANES), 0) + base < count
            rows = jnp.where(live, rows, 0.0)
            scaled = (rows * rows[:, members + 1 : members + 2]).astype(jnp.bfloat16)
            return total + lax.dot_general(
                rows.astype(jnp.bfloat16), scaled, TN, preferred_element_type=jnp.float32
            )

        gram[t] = lax.fori_loop(
            0, (count + LANES - 1) // LANES, chunk, jnp.zeros((LANES, LANES), jnp.float32)
        )
        return carry

    lax.fori_loop(0, share, tile, 0)

    copies = LANES // share

    def in_lanes(m):
        return jnp.concatenate([gram[:, m, :]] * copies, axis=0).T[:members]

    row_id = lax.broadcasted_iota(jnp.int32, (members, LANES), 0)
    for m in range(members):
        chol[m] = in_lanes(m) + jnp.where(row_id == m, members - 1.0, 0.0)
    rhs = in_lanes(members)

    width = 4
    for p in range(members // width):
        low = p * width // 8 * 8
        columns = [chol[p * width + q, low:, :] for q in range(width)]

        def eliminate(j, cols, p=p, low=low):
            left = chol[j, low:, :]
            return tuple(
                cols[q] - left * left[p * width + q - low : p * width + q - low + 1]
                for q in range(width)
            )

        columns = list(lax.fori_loop(0, p * width, eliminate, tuple(columns)))
        for q in range(width):
            at = p * width + q - low
            columns[q] = columns[q] * lax.rsqrt(columns[q][at : at + 1])
            for later in range(q + 1, width):
                spot = p * width + later - low
                columns[later] = columns[later] - columns[q] * columns[q][spot : spot + 1]
            chol[p * width + q, low:, :] = columns[q]

    for p in range(members // width):
        high = (p * width // 8 + 1) * 8
        ids = row_id[:high]
        rows = [jnp.where(ids == p * width + q, 1.0, 0.0) for q in range(width)]

        def substitute(j, rows, p=p, high=high):
            solved = inv[j, :high, :]
            group = chol[j, pl.ds(p * width // 8 * 8, 8), :]
            at = p * width % 8
            return tuple(
                rows[q] - solved * group[at + q : at + q + 1] for q in range(width)
            )

        rows = list(lax.fori_loop(0, p * width, substitute, tuple(rows)))
        for q in range(width):
            n = p * width + q
            rows[q] = rows[q] / chol[n, n : n + 1, :]
            for later in range(q + 1, width):
                spot = p * width + later
                rows[later] = rows[later] - rows[q] * chol[n, spot : spot + 1, :]
            inv[n, :high, :] = rows[q]
            if high < members:
                inv[n, high:, :] = jnp.zeros((members - high, LANES), jnp.float32)

    def apply(n, mean_weight):
        solved = inv[n]
        return mean_weight + solved * jnp.sum(solved * rhs, axis=0, keepdims=True)

    mean_weight = lax.fori_loop(0, members, apply, jnp.zeros((members, LANES), jnp.float32))
    root = float(members - 1) ** 0.5
    for n in range(members):
        weights = root * inv[n] + mean_weight
        mixed = weights + (1.0 - jnp.sum(weights, axis=0, keepdims=True)) * (1.0 / members)
        wide[:, n, :] = mixed.T[:share]
    half = members // 2
    out_ref[...] = jnp.concatenate([wide[:, :half], wide[:, half:]], axis=2).astype(jnp.bfloat16)


def update_kernel(snap_ref, snap_mix_ref, field_ref, field_mix_ref, smooth_ref, analysis_ref):
    owners, tiles, own, cols = field_ref.shape

    def tile(t, carry):
        smooth_ref[t] = jnp.dot(
            snap_mix_ref[t],
            snap_ref[:, t].reshape(owners * own, cols),
            preferred_element_type=jnp.float32,
        ).astype(jnp.bfloat16)
        analysis_ref[t] = jnp.dot(
            field_mix_ref[t],
            field_ref[:, t].reshape(owners * own, cols),
            preferred_element_type=jnp.float32,
        ).astype(jnp.bfloat16)
        return carry

    lax.fori_loop(0, tiles, tile, 0, unroll=4)


MESH = pl.DeviceIdType.MESH
CHUNKS = 4


def gather_kernel(block_ref, out_ref, own_sem, send_sem, recv_sem, pass_send, pass_recv):
    lag, core = lax.axis_index("lag"), lax.axis_index("member")
    lags = lax.axis_size("lag")
    size = block_ref.shape[0] // CHUNKS
    other = {"member": 1 - core}
    barrier = pltpu.get_barrier_semaphore()
    for d in range(1, lags):
        pl.semaphore_signal(
            barrier, inc=1, device_id={"lag": lax.rem(lag + d, lags)}, device_id_type=MESH
        )
    pl.semaphore_signal(barrier, inc=1, device_id=other, device_id_type=MESH)
    pl.semaphore_wait(barrier, lags)
    mine = lag * 2 + core
    keep = pltpu.make_async_copy(block_ref, out_ref.at[mine], own_sem)
    keep.start()
    across = []
    for c in range(CHUNKS):
        for d in range(1, lags):
            copy = pltpu.make_async_remote_copy(
                src_ref=block_ref.at[pl.ds(c * size, size)],
                dst_ref=out_ref.at[mine, pl.ds(c * size, size)],
                send_sem=send_sem.at[d, c],
                recv_sem=recv_sem.at[d, c],
                device_id={"lag": lax.rem(lag + d, lags)},
                device_id_type=MESH,
            )
            copy.start()
            across.append((c, d, copy))
    beside = []
    for c in range(CHUNKS):
        copy = pltpu.make_async_remote_copy(
            src_ref=block_ref.at[pl.ds(c * size, size)],
            dst_ref=out_ref.at[mine, pl.ds(c * size, size)],
            send_sem=pass_send.at[0, c],
            recv_sem=pass_recv.at[0, c],
            device_id=other,
            device_id_type=MESH,
        )
        copy.start()
        beside.append(copy)
    for c, d, copy in across:
        copy.wait_recv()
        slot = lax.rem(lag + lags - d, lags) * 2 + core
        onward = pltpu.make_async_remote_copy(
            src_ref=out_ref.at[slot, pl.ds(c * size, size)],
            dst_ref=out_ref.at[slot, pl.ds(c * size, size)],
            send_sem=pass_send.at[d, c],
            recv_sem=pass_recv.at[d, c],
            device_id=other,
            device_id_type=MESH,
        )
        onward.start()
        beside.append(onward)
    for c, d, copy in across:
        copy.wait_send()
    for copy in beside:
        copy.wait()
    keep.wait()


def group_gather(block, collective_id):
    lags = lax.axis_size("lag")
    sems = pltpu.SemaphoreType.DMA((lags, CHUNKS))
    return pl.pallas_call(
        gather_kernel,
        out_shape=jax.ShapeDtypeStruct((lags * 2,) + block.shape, block.dtype),
        in_specs=[pl.BlockSpec(memory_space=pl.ANY)],
        out_specs=pl.BlockSpec(memory_space=pl.ANY),
        scratch_shapes=[pltpu.SemaphoreType.DMA, sems, sems, sems, sems],
        compiler_params=pltpu.CompilerParams(collective_id=collective_id, has_side_effects=True),
    )(block)


def halo_kernel(block_ref, before_ref, after_ref, send_sem, recv_sem, pass_send, pass_recv):
    region, core = lax.axis_index("region"), lax.axis_index("member")
    regions = lax.axis_size("region")
    half = block_ref.shape[0] // 2
    size = half // 2
    other = {"member": 1 - core}
    has_before = region > 0
    has_after = region < regions - 1
    barrier = pltpu.get_barrier_semaphore()
    pl.semaphore_signal(barrier, inc=1, device_id=other, device_id_type=MESH)

    @pl.when(has_before)
    def _():
        pl.semaphore_signal(
            barrier, inc=1, device_id={"region": region - 1}, device_id_type=MESH
        )

    @pl.when(has_after)
    def _():
        pl.semaphore_signal(
            barrier, inc=1, device_id={"region": region + 1}, device_id_type=MESH
        )

    peers = 1 + has_before.astype(jnp.int32) + has_after.astype(jnp.int32)
    pl.semaphore_wait(barrier, peers)

    def rows(c):
        return pl.ds(pl.multiple_of(core * half + c * size, 16), size)

    def to_side(side, c):
        return pltpu.make_async_remote_copy(
            src_ref=block_ref.at[rows(c)],
            dst_ref=(before_ref, after_ref)[side].at[rows(c)],
            send_sem=send_sem.at[side, c],
            recv_sem=recv_sem.at[side, c],
            device_id={"region": region + 1 - 2 * side},
            device_id_type=MESH,
        )

    def onward(side, c):
        ref = (before_ref, after_ref)[side]
        return pltpu.make_async_remote_copy(
            src_ref=ref.at[rows(c)],
            dst_ref=ref.at[rows(c)],
            send_sem=pass_send.at[side, c],
            recv_sem=pass_recv.at[side, c],
            device_id=other,
            device_id_type=MESH,
        )

    sends = (has_after, has_before)
    receives = (has_before, has_after)
    for side in range(2):

        @pl.when(sends[side])
        def _(side=side):
            for c in range(2):
                to_side(side, c).start()

    for side, ref in enumerate((before_ref, after_ref)):

        @pl.when(jnp.logical_not(receives[side]))
        def _(ref=ref):
            ref[...] = jnp.zeros_like(ref)

    for c in range(2):
        for side in range(2):

            @pl.when(receives[side])
            def _(side=side, c=c):
                to_side(side, c).wait_recv()
                onward(side, c).start()

    for side in range(2):

        @pl.when(sends[side])
        def _(side=side):
            for c in range(2):
                to_side(side, c).wait_send()

        @pl.when(receives[side])
        def _(side=side):
            for c in range(2):
                onward(side, c).wait()


def sample_halo(block, collective_id):
    sems = pltpu.SemaphoreType.DMA((2, 2))
    vmem = pl.BlockSpec(memory_space=pltpu.VMEM)
    shape = jax.ShapeDtypeStruct(block.shape, block.dtype)
    return pl.pallas_call(
        halo_kernel,
        out_shape=(shape, shape),
        in_specs=[vmem],
        out_specs=(vmem, vmem),
        scratch_shapes=[sems, sems, sems, sems],
        compiler_params=pltpu.CompilerParams(
            collective_id=collective_id, has_side_effects=True, vmem_limit_bytes=VMEM_BYTES
        ),
    )(block)


def local(
    snapshots, current, diffusivity, landmask, obs_cell, obs_value, obs_weight, tile_obs, tile_count
):
    sea_mask = landmask.astype(jnp.float32)
    field_now = current
    for substep in range(STEPS):
        padded = with_halo(field_now, (("region", 1),), 1)
        field_now = relax(padded, diffusivity, sea_mask)
    newest = field_now.astype(jnp.bfloat16)
    own_members = newest.shape[0]
    obs_count = obs_cell.shape[0]
    obs_info = jnp.stack([obs_value, obs_weight])
    window_info = with_halo(obs_info.astype(jnp.bfloat16), (("region", 1),), obs_count).astype(
        obs_info.dtype
    )
    group_size = lax.axis_size(("lag", "member"))
    group_rank = lax.axis_index(("lag", "member"))
    by_row = newest.transpose(1, 0, 2)
    everyone = group_gather(by_row, 1)
    members = group_size * own_members
    vmem, smem = pltpu.VMEM, pltpu.SMEM
    rows, cols = newest.shape[1:]
    sampled = vmem_call(
        sample_kernel,
        jax.ShapeDtypeStruct((members, obs_count), jnp.bfloat16),
        [pltpu.VMEM((rows * cols, LANES), jnp.float32), pltpu.VMEM((LANES, LANES), jnp.float32)],
        (smem, vmem),
        10**8,
    )(obs_cell, everyone)
    before, after = sample_halo(sampled, 2)
    share = tile_obs.shape[0] // group_size
    first_tile = group_rank * share
    my_index = lax.dynamic_slice_in_dim(tile_obs, first_tile, share, 0).reshape(-1)
    my_count = lax.dynamic_slice_in_dim(tile_count, first_tile, share, 0)
    mine = vmem_call(
        mixing_kernel,
        jax.ShapeDtypeStruct((share, members // 2, 2 * members), jnp.bfloat16),
        [
            pltpu.VMEM((3 * obs_count, LANES), jnp.float32),
            pltpu.VMEM((tile_obs.shape[1], LANES), jnp.float32),
            pltpu.VMEM((share, LANES, LANES), jnp.float32),
            pltpu.VMEM((members, members, LANES), jnp.float32),
            pltpu.VMEM((members, members, LANES), jnp.float32),
            pltpu.VMEM((share, members, members), jnp.float32),
        ],
        (smem, smem, vmem, vmem, vmem, vmem),
        10**9,
    )(my_count, my_index, before, sampled, after, window_info.reshape(2, -1, LANES))
    mixing = group_gather(mine, 3)
    mixing = mixing.reshape(-1, members // 2, 2 * members)
    member_rank = lax.axis_index("member")
    half_members = snapshots.shape[1]
    snap_mix = lax.dynamic_slice_in_dim(mixing, member_rank * members, members, 2)
    first_member = group_rank * own_members
    field_mix = lax.dynamic_slice(
        mixing,
        (0, first_member % half_members, first_member // half_members * members),
        (mixing.shape[0], own_members, members),
    )
    snaps = lax.all_gather(snapshots[0].transpose(1, 0, 2), "member", axis=0)
    smoothed, analysis = vmem_call(
        update_kernel,
        (
            jax.ShapeDtypeStruct((rows, half_members, cols), jnp.bfloat16),
            jax.ShapeDtypeStruct((rows, own_members, cols), jnp.bfloat16),
        ),
        [],
        (vmem,) * 4,
        10**8,
    )(snaps, snap_mix, everyone, field_mix)
    return (smoothed.transpose(1, 0, 2)[None], analysis.transpose(1, 0, 2))


def solution(mesh):
    placed = (
        P(("groups", "lag"), "member", "region", None),
        P(("groups", "lag", "member"), "region", None),
        P("region", None),
        P("region", None),
        P(("groups", "region")),
        P(("groups", "region")),
        P(("groups", "region")),
        P(("groups", "region"), None),
        P(("groups", "region")),
    )
    return jax.shard_map(
        local,
        mesh=mesh,
        in_specs=placed,
        out_specs=(
            P(("groups", "lag"), "member", "region", None),
            P(("groups", "lag", "member"), "region", None),
        ),
        check_vma=False,
    )
```

```python
import functools

import jax
import jax.numpy as jnp
from jax import lax
from jax.experimental import pallas as pl
from jax.experimental.pallas import tpu as pltpu
from jax.sharding import PartitionSpec as P

STEPS = 2
LANES = 128
VMEM_BYTES = 56 * 1024 * 1024


def relax(padded, diffusion, sea_mask):
    centre = padded[:, 1:-1]
    upper_row = padded[:, :-2]
    lower_row = padded[:, 2:]
    right_cell = jnp.roll(centre, 1, axis=2)
    left_cell = jnp.roll(centre, -1, axis=2)
    return sea_mask * (
        centre + diffusion * (upper_row + lower_row + right_cell + left_cell - 4.0 * centre)
    )


NT = (((1,), (1,)), ((), ()))
TN = (((0,), (0,)), ((), ()))


def identity():
    row = lax.broadcasted_iota(jnp.int32, (LANES, LANES), 0)
    col = lax.broadcasted_iota(jnp.int32, (LANES, LANES), 1)
    return (row == col).astype(jnp.bfloat16)


def vmem_call(kernel, out_shape, scratch_shapes, in_spaces, flops):
    return pl.pallas_call(
        kernel,
        out_shape=out_shape,
        in_specs=[pl.BlockSpec(memory_space=space) for space in in_spaces],
        out_specs=jax.tree.map(lambda _: pl.BlockSpec(memory_space=pltpu.VMEM), out_shape),
        scratch_shapes=scratch_shapes,
        compiler_params=pltpu.CompilerParams(vmem_limit_bytes=VMEM_BYTES),
        cost_estimate=pl.CostEstimate(flops=flops, bytes_accessed=1 << 22, transcendentals=0),
    )


def sample_kernel(cell_ref, field_ref, out_ref, table, picked):
    owners, rows, own, cols = field_ref.shape
    members = owners * own
    eye = identity()

    def build(r, carry):
        part = field_ref[:, r].reshape(members, cols)
        table[pl.ds(pl.multiple_of(r * cols, cols), cols), :members] = lax.dot_general(
            eye, part, NT, preferred_element_type=jnp.float32
        )
        return carry

    lax.fori_loop(0, rows, build, 0, unroll=4)
    picked[:, members:] = jnp.zeros((LANES, LANES - members), jnp.float32)

    def block(b, carry):
        base = pl.multiple_of(b * LANES, LANES)

        def rows16(g, inner):
            found = [
                table[pl.ds(cell_ref[base + g * 16 + q], 1), :members] for q in range(16)
            ]
            for q in range(16):
                picked[pl.ds(g * 16 + q, 1), :members] = found[q]
            return inner

        lax.fori_loop(0, LANES // 16, rows16, 0, unroll=True)
        flipped = picked[...].T
        out_ref[:, pl.ds(base, LANES)] = flipped[:members].astype(jnp.bfloat16)
        return carry

    lax.fori_loop(0, cell_ref.shape[0] // LANES, block, 0)


def mixing_kernel(
    count_ref, index_ref, before_ref, own_ref, after_ref, info_ref, out_ref,
    table, picked, gram, chol, inv, wide,
):
    share = count_ref.shape[0]
    entries = index_ref.shape[0] // share
    members, obs = own_ref.shape
    blocks = obs // LANES
    eye = identity()

    for part, ref in enumerate((before_ref, own_ref, after_ref)):

        def build(b, carry, part=part, ref=ref):
            sample = ref[:, pl.ds(pl.multiple_of(b * LANES, LANES), LANES)].astype(jnp.float32)
            mean = jnp.sum(sample, axis=0, keepdims=True) * (1.0 / members)
            value = info_ref[0, pl.ds(part * blocks + b, 1), :]
            weight = info_ref[1, pl.ds(part * blocks + b, 1), :]
            row = lax.broadcasted_iota(jnp.int32, (LANES - members, LANES), 0)
            extra = jnp.where(row == 0, value - mean, jnp.where(row == 1, weight, 0.0))
            rows = jnp.concatenate([sample - mean, extra], axis=0).astype(jnp.bfloat16)
            table[pl.ds(pl.multiple_of((part * blocks + b) * LANES, LANES), LANES), :] = (
                lax.dot_general(eye, rows, NT, preferred_element_type=jnp.float32)
            )
            return carry

        lax.fori_loop(0, blocks, build, 0, unroll=4)

    def tile(t, carry):
        count = count_ref[t]
        first = t * entries

        def rows16(g, inner):
            found = [table[pl.ds(index_ref[first + g * 16 + q], 1), :] for q in range(16)]
            for q in range(16):
                picked[pl.ds(g * 16 + q, 1), :] = found[q]
            return inner

        lax.fori_loop(0, (count + 15) // 16, rows16, 0)

        def chunk(c, total):
            base = pl.multiple_of(c * LANES, LANES)
            rows = picked[pl.ds(base, LANES), :]
            live = lax.broadcasted_iota(jnp.int32, (LANES, LANES), 0) + base < count
            rows = jnp.where(live, rows, 0.0)
            scaled = (rows * rows[:, members + 1 : members + 2]).astype(jnp.bfloat16)
            return total + lax.dot_general(
                rows.astype(jnp.bfloat16), scaled, TN, preferred_element_type=jnp.float32
            )

        gram[t] = lax.fori_loop(
            0, (count + LANES - 1) // LANES, chunk, jnp.zeros((LANES, LANES), jnp.float32)
        )
        return carry

    lax.fori_loop(0, share, tile, 0)

    def in_lanes(m):
        return gram[:, m, :].T[:members]

    row_id = lax.broadcasted_iota(jnp.int32, (members, share), 0)
    for m in range(members):
        chol[m] = in_lanes(m) + jnp.where(row_id == m, members - 1.0, 0.0)
    rhs = in_lanes(members)

    width = 4
    for p in range(members // width):
        low = p * width // 8 * 8
        columns = [chol[p * width + q, low:, :] for q in range(width)]

        def eliminate(j, cols, p=p, low=low):
            left = chol[j, low:, :]
            return tuple(
                cols[q] - left * left[p * width + q - low : p * width + q - low + 1]
                for q in range(width)
            )

        columns = list(lax.fori_loop(0, p * width, eliminate, tuple(columns), unroll=4))
        for q in range(width):
            at = p * width + q - low
            columns[q] = columns[q] * lax.rsqrt(columns[q][at : at + 1])
            for later in range(q + 1, width):
                spot = p * width + later - low
                columns[later] = columns[later] - columns[q] * columns[q][spot : spot + 1]
            chol[p * width + q, low:, :] = columns[q]

    for p in range(members // width):
        high = (p * width // 8 + 1) * 8
        ids = row_id[:high]
        rows = [jnp.where(ids == p * width + q, 1.0, 0.0) for q in range(width)]

        def substitute(j, rows, p=p, high=high):
            solved = inv[j, :high, :]
            group = chol[j, pl.ds(p * width // 8 * 8, 8), :]
            at = p * width % 8
            return tuple(
                rows[q] - solved * group[at + q : at + q + 1] for q in range(width)
            )

        rows = list(lax.fori_loop(0, p * width, substitute, tuple(rows), unroll=4))
        for q in range(width):
            n = p * width + q
            rows[q] = rows[q] / chol[n, n : n + 1, :]
            for later in range(q + 1, width):
                spot = p * width + later
                rows[later] = rows[later] - rows[q] * chol[n, spot : spot + 1, :]
            inv[n, :high, :] = rows[q]
            if high < members:
                inv[n, high:, :] = jnp.zeros((members - high, share), jnp.float32)

    def apply(n, mean_weight):
        solved = inv[n]
        return mean_weight + solved * jnp.sum(solved * rhs, axis=0, keepdims=True)

    mean_weight = lax.fori_loop(0, members, apply, jnp.zeros((members, share), jnp.float32))
    root = float(members - 1) ** 0.5
    for n in range(members):
        weights = root * inv[n] + mean_weight
        mixed = weights + (1.0 - jnp.sum(weights, axis=0, keepdims=True)) * (1.0 / members)
        wide[:, n, :] = mixed.T
    half = members // 2
    out_ref[...] = jnp.concatenate([wide[:, :half], wide[:, half:]], axis=2).astype(jnp.bfloat16)


def update_kernel(snap_ref, snap_mix_ref, field_ref, field_mix_ref, smooth_ref, analysis_ref):
    owners, tiles, own, cols = field_ref.shape

    def tile(t, carry):
        smooth_ref[t] = jnp.dot(
            snap_mix_ref[t],
            snap_ref[:, t].reshape(owners * own, cols),
            preferred_element_type=jnp.float32,
        ).astype(jnp.bfloat16)
        analysis_ref[t] = jnp.dot(
            field_mix_ref[t],
            field_ref[:, t].reshape(owners * own, cols),
            preferred_element_type=jnp.float32,
        ).astype(jnp.bfloat16)
        return carry

    lax.fori_loop(0, tiles, tile, 0, unroll=4)


MESH = pl.DeviceIdType.MESH
CHUNKS = 4


def gather_kernel(block_ref, out_ref, own_sem, send_sem, recv_sem, pass_send, pass_recv):
    lag, core = lax.axis_index("lag"), lax.axis_index("member")
    lags = lax.axis_size("lag")
    size = block_ref.shape[0] // CHUNKS
    other = {"member": 1 - core}
    barrier = pltpu.get_barrier_semaphore()
    for d in range(1, lags):
        pl.semaphore_signal(
            barrier, inc=1, device_id={"lag": lax.rem(lag + d, lags)}, device_id_type=MESH
        )
    pl.semaphore_signal(barrier, inc=1, device_id=other, device_id_type=MESH)
    pl.semaphore_wait(barrier, lags)
    mine = lag * 2 + core
    keep = pltpu.make_async_copy(block_ref, out_ref.at[mine], own_sem)
    keep.start()
    across = []
    for c in range(CHUNKS):
        for d in range(1, lags):
            copy = pltpu.make_async_remote_copy(
                src_ref=block_ref.at[pl.ds(c * size, size)],
                dst_ref=out_ref.at[mine, pl.ds(c * size, size)],
                send_sem=send_sem.at[d, c],
                recv_sem=recv_sem.at[d, c],
                device_id={"lag": lax.rem(lag + d, lags)},
                device_id_type=MESH,
            )
            copy.start()
            across.append((c, d, copy))
    beside = []
    for c in range(CHUNKS):
        copy = pltpu.make_async_remote_copy(
            src_ref=block_ref.at[pl.ds(c * size, size)],
            dst_ref=out_ref.at[mine, pl.ds(c * size, size)],
            send_sem=pass_send.at[0, c],
            recv_sem=pass_recv.at[0, c],
            device_id=other,
            device_id_type=MESH,
        )
        copy.start()
        beside.append(copy)
    for c, d, copy in across:
        copy.wait_recv()
        slot = lax.rem(lag + lags - d, lags) * 2 + core
        onward = pltpu.make_async_remote_copy(
            src_ref=out_ref.at[slot, pl.ds(c * size, size)],
            dst_ref=out_ref.at[slot, pl.ds(c * size, size)],
            send_sem=pass_send.at[d, c],
            recv_sem=pass_recv.at[d, c],
            device_id=other,
            device_id_type=MESH,
        )
        onward.start()
        beside.append(onward)
    for c, d, copy in across:
        copy.wait_send()
    for copy in beside:
        copy.wait()
    keep.wait()


def group_gather(block, collective_id):
    lags = lax.axis_size("lag")
    sems = pltpu.SemaphoreType.DMA((lags, CHUNKS))
    return pl.pallas_call(
        gather_kernel,
        out_shape=jax.ShapeDtypeStruct((lags * 2,) + block.shape, block.dtype),
        in_specs=[pl.BlockSpec(memory_space=pl.ANY)],
        out_specs=pl.BlockSpec(memory_space=pl.ANY),
        scratch_shapes=[pltpu.SemaphoreType.DMA, sems, sems, sems, sems],
        compiler_params=pltpu.CompilerParams(collective_id=collective_id, has_side_effects=True),
    )(block)


def halo_kernel(block_ref, before_ref, after_ref, send_sem, recv_sem, pass_send, pass_recv):
    region, core = lax.axis_index("region"), lax.axis_index("member")
    regions = lax.axis_size("region")
    half = block_ref.shape[0] // 2
    size = half // 2
    other = {"member": 1 - core}
    has_before = region > 0
    has_after = region < regions - 1
    barrier = pltpu.get_barrier_semaphore()
    pl.semaphore_signal(barrier, inc=1, device_id=other, device_id_type=MESH)

    @pl.when(has_before)
    def _():
        pl.semaphore_signal(
            barrier, inc=1, device_id={"region": region - 1}, device_id_type=MESH
        )

    @pl.when(has_after)
    def _():
        pl.semaphore_signal(
            barrier, inc=1, device_id={"region": region + 1}, device_id_type=MESH
        )

    peers = 1 + has_before.astype(jnp.int32) + has_after.astype(jnp.int32)
    pl.semaphore_wait(barrier, peers)

    def rows(c):
        return pl.ds(pl.multiple_of(core * half + c * size, 16), size)

    def to_side(side, c):
        return pltpu.make_async_remote_copy(
            src_ref=block_ref.at[rows(c)],
            dst_ref=(before_ref, after_ref)[side].at[rows(c)],
            send_sem=send_sem.at[side, c],
            recv_sem=recv_sem.at[side, c],
            device_id={"region": region + 1 - 2 * side},
            device_id_type=MESH,
        )

    def onward(side, c):
        ref = (before_ref, after_ref)[side]
        return pltpu.make_async_remote_copy(
            src_ref=ref.at[rows(c)],
            dst_ref=ref.at[rows(c)],
            send_sem=pass_send.at[side, c],
            recv_sem=pass_recv.at[side, c],
            device_id=other,
            device_id_type=MESH,
        )

    sends = (has_after, has_before)
    receives = (has_before, has_after)
    for side in range(2):

        @pl.when(sends[side])
        def _(side=side):
            for c in range(2):
                to_side(side, c).start()

    for side, ref in enumerate((before_ref, after_ref)):

        @pl.when(jnp.logical_not(receives[side]))
        def _(ref=ref):
            ref[...] = jnp.zeros_like(ref)

    for c in range(2):
        for side in range(2):

            @pl.when(receives[side])
            def _(side=side, c=c):
                to_side(side, c).wait_recv()
                onward(side, c).start()

    for side in range(2):

        @pl.when(sends[side])
        def _(side=side):
            for c in range(2):
                to_side(side, c).wait_send()

        @pl.when(receives[side])
        def _(side=side):
            for c in range(2):
                onward(side, c).wait()


def sample_halo(block, collective_id):
    sems = pltpu.SemaphoreType.DMA((2, 2))
    vmem = pl.BlockSpec(memory_space=pltpu.VMEM)
    shape = jax.ShapeDtypeStruct(block.shape, block.dtype)
    return pl.pallas_call(
        halo_kernel,
        out_shape=(shape, shape),
        in_specs=[vmem],
        out_specs=(vmem, vmem),
        scratch_shapes=[sems, sems, sems, sems],
        compiler_params=pltpu.CompilerParams(
            collective_id=collective_id, has_side_effects=True, vmem_limit_bytes=VMEM_BYTES
        ),
    )(block)


def local(
    snapshots, current, diffusivity, landmask, obs_cell, obs_value, obs_weight, tile_obs, tile_count
):
    sea_mask = landmask.astype(jnp.float32)
    own_members, rows, cols = current.shape
    depth = STEPS

    def edge(low, margin):
        return jnp.concatenate(
            [
                current[:, low : low + depth].reshape(-1),
                diffusivity[margin : margin + depth - 1].reshape(-1),
                sea_mask[margin : margin + depth - 1].reshape(-1),
                obs_value,
                obs_weight,
            ]
        ).reshape(-1, cols)

    size = lax.axis_size("region")
    up = [(i, i + 1) for i in range(size - 1)]
    down = [(j, i) for i, j in up]
    before = lax.ppermute(edge(rows - depth, rows - depth + 1), "region", up)
    after = lax.ppermute(edge(0, 0), "region", down)
    cut = own_members * depth
    pieces = [
        (
            part[:cut].reshape(own_members, depth, cols),
            part[cut : cut + depth - 1],
            part[cut + depth - 1 : cut + 2 * (depth - 1)],
            part[cut + 2 * (depth - 1) :].reshape(2, -1, cols),
        )
        for part in (before, after)
    ]
    field_now = jnp.concatenate([pieces[0][0], current, pieces[1][0]], axis=1)
    diffusion = jnp.concatenate([pieces[0][1], diffusivity, pieces[1][1]], axis=0)
    wide_mask = jnp.concatenate([pieces[0][2], sea_mask, pieces[1][2]], axis=0)
    for substep in range(depth):
        span = slice(substep, diffusion.shape[0] - substep)
        field_now = relax(field_now, diffusion[span], wide_mask[span])
    newest = field_now.astype(jnp.bfloat16)
    obs_count = obs_cell.shape[0]
    own_info = jnp.stack([obs_value, obs_weight]).reshape(2, -1, cols)
    window_info = jnp.concatenate([pieces[0][3], own_info, pieces[1][3]], axis=1)
    group_size = lax.axis_size(("lag", "member"))
    group_rank = lax.axis_index(("lag", "member"))
    by_row = newest.transpose(1, 0, 2)
    everyone = group_gather(by_row, 1)
    members = group_size * own_members
    vmem, smem = pltpu.VMEM, pltpu.SMEM
    sampled = vmem_call(
        sample_kernel,
        jax.ShapeDtypeStruct((members, obs_count), jnp.bfloat16),
        [pltpu.VMEM((rows * cols, LANES), jnp.float32), pltpu.VMEM((LANES, LANES), jnp.float32)],
        (smem, vmem),
        10**8,
    )(obs_cell, everyone)
    before, after = sample_halo(sampled, 2)
    share = tile_obs.shape[0] // group_size
    first_tile = group_rank * share
    my_index = lax.dynamic_slice_in_dim(tile_obs, first_tile, share, 0).reshape(-1)
    my_count = lax.dynamic_slice_in_dim(tile_count, first_tile, share, 0)
    mine = vmem_call(
        mixing_kernel,
        jax.ShapeDtypeStruct((share, members // 2, 2 * members), jnp.bfloat16),
        [
            pltpu.VMEM((3 * obs_count, LANES), jnp.float32),
            pltpu.VMEM((tile_obs.shape[1], LANES), jnp.float32),
            pltpu.VMEM((share, LANES, LANES), jnp.float32),
            pltpu.VMEM((members, members, share), jnp.float32),
            pltpu.VMEM((members, members, share), jnp.float32),
            pltpu.VMEM((share, members, members), jnp.float32),
        ],
        (smem, smem, vmem, vmem, vmem, vmem),
        10**9,
    )(my_count, my_index, before, sampled, after, window_info)
    mixing = group_gather(mine, 3)
    mixing = mixing.reshape(-1, members // 2, 2 * members)
    member_rank = lax.axis_index("member")
    half_members = snapshots.shape[1]
    snap_mix = lax.dynamic_slice_in_dim(mixing, member_rank * members, members, 2)
    first_member = group_rank * own_members
    field_mix = lax.dynamic_slice(
        mixing,
        (0, first_member % half_members, first_member // half_members * members),
        (mixing.shape[0], own_members, members),
    )
    snaps = lax.all_gather(snapshots[0].transpose(1, 0, 2), "member", axis=0)
    smoothed, analysis = vmem_call(
        update_kernel,
        (
            jax.ShapeDtypeStruct((rows, half_members, cols), jnp.bfloat16),
            jax.ShapeDtypeStruct((rows, own_members, cols), jnp.bfloat16),
        ),
        [],
        (vmem,) * 4,
        10**8,
    )(snaps, snap_mix, everyone, field_mix)
    return (smoothed.transpose(1, 0, 2)[None], analysis.transpose(1, 0, 2))


def solution(mesh):
    placed = (
        P(("groups", "lag"), "member", "region", None),
        P(("groups", "lag", "member"), "region", None),
        P("region", None),
        P("region", None),
        P(("groups", "region")),
        P(("groups", "region")),
        P(("groups", "region")),
        P(("groups", "region"), None),
        P(("groups", "region")),
    )
    return jax.shard_map(
        local,
        mesh=mesh,
        in_specs=placed,
        out_specs=(
            P(("groups", "lag"), "member", "region", None),
            P(("groups", "lag", "member"), "region", None),
        ),
        check_vma=False,
    )
```

```python
import functools

import jax
import jax.numpy as jnp
from jax import lax
from jax.experimental import pallas as pl
from jax.experimental.pallas import tpu as pltpu
from jax.sharding import PartitionSpec as P

STEPS = 2
LANES = 128
VMEM_BYTES = 56 * 1024 * 1024


def relax(padded, diffusion, sea_mask):
    centre = padded[:, 1:-1]
    upper_row = padded[:, :-2]
    lower_row = padded[:, 2:]
    right_cell = jnp.roll(centre, 1, axis=2)
    left_cell = jnp.roll(centre, -1, axis=2)
    return sea_mask * (
        centre + diffusion * (upper_row + lower_row + right_cell + left_cell - 4.0 * centre)
    )


NT = (((1,), (1,)), ((), ()))
TN = (((0,), (0,)), ((), ()))


def identity():
    row = lax.broadcasted_iota(jnp.int32, (LANES, LANES), 0)
    col = lax.broadcasted_iota(jnp.int32, (LANES, LANES), 1)
    return (row == col).astype(jnp.bfloat16)


def vmem_call(kernel, out_shape, scratch_shapes, in_spaces, flops):
    return pl.pallas_call(
        kernel,
        out_shape=out_shape,
        in_specs=[pl.BlockSpec(memory_space=space) for space in in_spaces],
        out_specs=jax.tree.map(lambda _: pl.BlockSpec(memory_space=pltpu.VMEM), out_shape),
        scratch_shapes=scratch_shapes,
        compiler_params=pltpu.CompilerParams(vmem_limit_bytes=VMEM_BYTES),
        cost_estimate=pl.CostEstimate(flops=flops, bytes_accessed=1 << 22, transcendentals=0),
    )


def sample_kernel(cell_ref, field_ref, out_ref, table, picked):
    owners, rows, own, cols = field_ref.shape
    members = owners * own
    eye = identity()

    def build(r, carry):
        part = field_ref[:, r].reshape(members, cols)
        table[pl.ds(pl.multiple_of(r * cols, cols), cols), :members] = lax.dot_general(
            eye, part, NT, preferred_element_type=jnp.float32
        )
        return carry

    lax.fori_loop(0, rows, build, 0, unroll=4)
    picked[:, members:] = jnp.zeros((LANES, LANES - members), jnp.float32)

    def block(b, carry):
        base = pl.multiple_of(b * LANES, LANES)

        def rows16(g, inner):
            found = [
                table[pl.ds(cell_ref[base + g * 16 + q], 1), :members] for q in range(16)
            ]
            for q in range(16):
                picked[pl.ds(g * 16 + q, 1), :members] = found[q]
            return inner

        lax.fori_loop(0, LANES // 16, rows16, 0, unroll=True)
        flipped = picked[...].T
        out_ref[:, pl.ds(base, LANES)] = flipped[:members].astype(jnp.bfloat16)
        return carry

    lax.fori_loop(0, cell_ref.shape[0] // LANES, block, 0)


def mixing_kernel(
    count_ref, index_ref, window_ref, info_ref, out_ref,
    table, picked, gram, chol, inv, wide,
):
    share = count_ref.shape[0]
    entries = index_ref.shape[0] // share
    members, obs = window_ref.shape[2:]
    blocks = obs // LANES
    eye = identity()

    for part in range(6):

        def build(b, carry, part=part):
            start = pl.multiple_of(b * LANES, LANES)
            sample = window_ref[part // 2, part % 2, :, pl.ds(start, LANES)].astype(jnp.float32)
            mean = jnp.sum(sample, axis=0, keepdims=True) * (1.0 / members)
            value = info_ref[0, pl.ds(part * blocks + b, 1), :]
            weight = info_ref[1, pl.ds(part * blocks + b, 1), :]
            row = lax.broadcasted_iota(jnp.int32, (LANES - members, LANES), 0)
            extra = jnp.where(row == 0, value - mean, jnp.where(row == 1, weight, 0.0))
            rows = jnp.concatenate([sample - mean, extra], axis=0).astype(jnp.bfloat16)
            table[pl.ds(pl.multiple_of((part * blocks + b) * LANES, LANES), LANES), :] = (
                lax.dot_general(eye, rows, NT, preferred_element_type=jnp.float32)
            )
            return carry

        lax.fori_loop(0, blocks, build, 0, unroll=4)

    def tile(t, carry):
        count = count_ref[t]
        first = t * entries

        def rows16(g, inner):
            found = [table[pl.ds(index_ref[first + g * 16 + q], 1), :] for q in range(16)]
            for q in range(16):
                picked[pl.ds(g * 16 + q, 1), :] = found[q]
            return inner

        lax.fori_loop(0, (count + 15) // 16, rows16, 0)

        def chunk(c, total):
            base = pl.multiple_of(c * LANES, LANES)
            rows = picked[pl.ds(base, LANES), :]
            live = lax.broadcasted_iota(jnp.int32, (LANES, LANES), 0) + base < count
            rows = jnp.where(live, rows, 0.0)
            scaled = (rows * rows[:, members + 1 : members + 2]).astype(jnp.bfloat16)
            return total + lax.dot_general(
                rows.astype(jnp.bfloat16), scaled, TN, preferred_element_type=jnp.float32
            )

        gram[t] = lax.fori_loop(
            0, (count + LANES - 1) // LANES, chunk, jnp.zeros((LANES, LANES), jnp.float32)
        )
        return carry

    lax.fori_loop(0, share, tile, 0)

    def in_lanes(m):
        return gram[:, m, :].T[:members]

    row_id = lax.broadcasted_iota(jnp.int32, (members, share), 0)
    for m in range(members):
        chol[m] = in_lanes(m) + jnp.where(row_id == m, members - 1.0, 0.0)
    rhs = in_lanes(members)

    width = 4
    for p in range(members // width):
        low = p * width // 8 * 8
        columns = [chol[p * width + q, low:, :] for q in range(width)]

        def eliminate(j, cols, p=p, low=low):
            left = chol[j, low:, :]
            return tuple(
                cols[q] - left * left[p * width + q - low : p * width + q - low + 1]
                for q in range(width)
            )

        columns = list(lax.fori_loop(0, p * width, eliminate, tuple(columns), unroll=4))
        for q in range(width):
            at = p * width + q - low
            columns[q] = columns[q] * lax.rsqrt(columns[q][at : at + 1])
            for later in range(q + 1, width):
                spot = p * width + later - low
                columns[later] = columns[later] - columns[q] * columns[q][spot : spot + 1]
            chol[p * width + q, low:, :] = columns[q]

    for p in range(members // width):
        high = (p * width // 8 + 1) * 8
        ids = row_id[:high]
        rows = [jnp.where(ids == p * width + q, 1.0, 0.0) for q in range(width)]

        def substitute(j, rows, p=p, high=high):
            solved = inv[j, :high, :]
            group = chol[j, pl.ds(p * width // 8 * 8, 8), :]
            at = p * width % 8
            return tuple(
                rows[q] - solved * group[at + q : at + q + 1] for q in range(width)
            )

        rows = list(lax.fori_loop(0, p * width, substitute, tuple(rows), unroll=4))
        for q in range(width):
            n = p * width + q
            rows[q] = rows[q] / chol[n, n : n + 1, :]
            for later in range(q + 1, width):
                spot = p * width + later
                rows[later] = rows[later] - rows[q] * chol[n, spot : spot + 1, :]
            inv[n, :high, :] = rows[q]
            if high < members:
                inv[n, high:, :] = jnp.zeros((members - high, share), jnp.float32)

    def apply(n, mean_weight):
        solved = inv[n]
        return mean_weight + solved * jnp.sum(solved * rhs, axis=0, keepdims=True)

    mean_weight = lax.fori_loop(0, members, apply, jnp.zeros((members, share), jnp.float32))
    root = float(members - 1) ** 0.5
    for n in range(members):
        weights = root * inv[n] + mean_weight
        mixed = weights + (1.0 - jnp.sum(weights, axis=0, keepdims=True)) * (1.0 / members)
        wide[:, n, :] = mixed.T
    half = members // 2
    out_ref[...] = jnp.concatenate([wide[:, :half], wide[:, half:]], axis=2).astype(jnp.bfloat16)


def update_kernel(snap_ref, snap_mix_ref, field_ref, field_mix_ref, smooth_ref, analysis_ref):
    owners, tiles, own, cols = field_ref.shape

    def tile(t, carry):
        smooth_ref[t] = jnp.dot(
            snap_mix_ref[t],
            snap_ref[:, t].reshape(owners * own, cols),
            preferred_element_type=jnp.float32,
        ).astype(jnp.bfloat16)
        analysis_ref[t] = jnp.dot(
            field_mix_ref[t],
            field_ref[:, t].reshape(owners * own, cols),
            preferred_element_type=jnp.float32,
        ).astype(jnp.bfloat16)
        return carry

    lax.fori_loop(0, tiles, tile, 0, unroll=4)


MESH = pl.DeviceIdType.MESH
CHUNKS = 4


def gather_kernel(block_ref, out_ref, own_sem, send_sem, recv_sem, pass_send, pass_recv):
    lag, core = lax.axis_index("lag"), lax.axis_index("member")
    lags = lax.axis_size("lag")
    size = block_ref.shape[0] // CHUNKS
    other = {"member": 1 - core}
    barrier = pltpu.get_barrier_semaphore()
    for d in range(1, lags):
        pl.semaphore_signal(
            barrier, inc=1, device_id={"lag": lax.rem(lag + d, lags)}, device_id_type=MESH
        )
    pl.semaphore_signal(barrier, inc=1, device_id=other, device_id_type=MESH)
    pl.semaphore_wait(barrier, lags)
    mine = lag * 2 + core
    keep = pltpu.make_async_copy(block_ref, out_ref.at[mine], own_sem)
    keep.start()
    across = []
    for c in range(CHUNKS):
        for d in range(1, lags):
            copy = pltpu.make_async_remote_copy(
                src_ref=block_ref.at[pl.ds(c * size, size)],
                dst_ref=out_ref.at[mine, pl.ds(c * size, size)],
                send_sem=send_sem.at[d, c],
                recv_sem=recv_sem.at[d, c],
                device_id={"lag": lax.rem(lag + d, lags)},
                device_id_type=MESH,
            )
            copy.start()
            across.append((c, d, copy))
    beside = []
    for c in range(CHUNKS):
        copy = pltpu.make_async_remote_copy(
            src_ref=block_ref.at[pl.ds(c * size, size)],
            dst_ref=out_ref.at[mine, pl.ds(c * size, size)],
            send_sem=pass_send.at[0, c],
            recv_sem=pass_recv.at[0, c],
            device_id=other,
            device_id_type=MESH,
        )
        copy.start()
        beside.append(copy)
    for c, d, copy in across:
        copy.wait_recv()
        slot = lax.rem(lag + lags - d, lags) * 2 + core
        onward = pltpu.make_async_remote_copy(
            src_ref=out_ref.at[slot, pl.ds(c * size, size)],
            dst_ref=out_ref.at[slot, pl.ds(c * size, size)],
            send_sem=pass_send.at[d, c],
            recv_sem=pass_recv.at[d, c],
            device_id=other,
            device_id_type=MESH,
        )
        onward.start()
        beside.append(onward)
    for c, d, copy in across:
        copy.wait_send()
    for copy in beside:
        copy.wait()
    keep.wait()


def group_gather(block, collective_id):
    lags = lax.axis_size("lag")
    sems = pltpu.SemaphoreType.DMA((lags, CHUNKS))
    return pl.pallas_call(
        gather_kernel,
        out_shape=jax.ShapeDtypeStruct((lags * 2,) + block.shape, block.dtype),
        in_specs=[pl.BlockSpec(memory_space=pl.ANY)],
        out_specs=pl.BlockSpec(memory_space=pl.ANY),
        scratch_shapes=[pltpu.SemaphoreType.DMA, sems, sems, sems, sems],
        compiler_params=pltpu.CompilerParams(collective_id=collective_id, has_side_effects=True),
    )(block)


def halo_kernel(block_ref, window_ref, own_send, own_recv, send_sem, recv_sem, pass_send, pass_recv):
    region, core = lax.axis_index("region"), lax.axis_index("member")
    regions = lax.axis_size("region")
    size = block_ref.shape[0] // 2
    other = {"member": 1 - core}
    has_before = region > 0
    has_after = region < regions - 1
    barrier = pltpu.get_barrier_semaphore()
    pl.semaphore_signal(barrier, inc=1, device_id=other, device_id_type=MESH)

    @pl.when(has_before)
    def _():
        pl.semaphore_signal(
            barrier, inc=1, device_id={"region": region - 1}, device_id_type=MESH
        )

    @pl.when(has_after)
    def _():
        pl.semaphore_signal(
            barrier, inc=1, device_id={"region": region + 1}, device_id_type=MESH
        )

    peers = 1 + has_before.astype(jnp.int32) + has_after.astype(jnp.int32)
    pl.semaphore_wait(barrier, peers)

    def rows(c):
        return pl.ds(c * size, size)

    def to_side(side, c):
        return pltpu.make_async_remote_copy(
            src_ref=block_ref.at[rows(c)],
            dst_ref=window_ref.at[2 * side, core, rows(c)],
            send_sem=send_sem.at[side, c],
            recv_sem=recv_sem.at[side, c],
            device_id={"region": region + 1 - 2 * side},
            device_id_type=MESH,
        )

    def onward(side, c):
        ref = window_ref.at[2 * side, core]
        return pltpu.make_async_remote_copy(
            src_ref=ref.at[rows(c)],
            dst_ref=ref.at[rows(c)],
            send_sem=pass_send.at[side, c],
            recv_sem=pass_recv.at[side, c],
            device_id=other,
            device_id_type=MESH,
        )

    sends = (has_after, has_before)
    receives = (has_before, has_after)
    for side in range(2):

        @pl.when(sends[side])
        def _(side=side):
            for c in range(2):
                to_side(side, c).start()

    beside = pltpu.make_async_remote_copy(
        src_ref=block_ref,
        dst_ref=window_ref.at[1, core],
        send_sem=own_send,
        recv_sem=own_recv,
        device_id=other,
        device_id_type=MESH,
    )
    beside.start()
    window_ref[1, core] = block_ref[...]
    for side in range(2):

        @pl.when(jnp.logical_not(receives[side]))
        def _(side=side):
            window_ref[2 * side] = jnp.zeros(window_ref.shape[1:], window_ref.dtype)

    for c in range(2):
        for side in range(2):

            @pl.when(receives[side])
            def _(side=side, c=c):
                to_side(side, c).wait_recv()
                onward(side, c).start()

    for side in range(2):

        @pl.when(sends[side])
        def _(side=side):
            for c in range(2):
                to_side(side, c).wait_send()

        @pl.when(receives[side])
        def _(side=side):
            for c in range(2):
                onward(side, c).wait()

    beside.wait()


def sample_halo(block, collective_id):
    sems = pltpu.SemaphoreType.DMA((2, 2))
    vmem = pl.BlockSpec(memory_space=pltpu.VMEM)
    shape = jax.ShapeDtypeStruct((3, 2) + block.shape, block.dtype)
    one = pltpu.SemaphoreType.DMA
    return pl.pallas_call(
        halo_kernel,
        out_shape=shape,
        in_specs=[vmem],
        out_specs=vmem,
        scratch_shapes=[one, one, sems, sems, sems, sems],
        compiler_params=pltpu.CompilerParams(
            collective_id=collective_id, has_side_effects=True, vmem_limit_bytes=VMEM_BYTES
        ),
    )(block)


def local(
    snapshots, current, diffusivity, landmask, obs_cell, obs_value, obs_weight, tile_obs, tile_count
):
    sea_mask = landmask.astype(jnp.float32)
    own_members, rows, cols = current.shape
    depth = STEPS

    def edge(low, margin):
        return jnp.concatenate(
            [
                current[:, low : low + depth].reshape(-1),
                diffusivity[margin : margin + depth - 1].reshape(-1),
                sea_mask[margin : margin + depth - 1].reshape(-1),
                obs_value,
                obs_weight,
            ]
        ).reshape(-1, cols)

    size = lax.axis_size("region")
    up = [(i, i + 1) for i in range(size - 1)]
    down = [(j, i) for i, j in up]
    before = lax.ppermute(edge(rows - depth, rows - depth + 1), "region", up)
    after = lax.ppermute(edge(0, 0), "region", down)
    cut = own_members * depth
    pieces = [
        (
            part[:cut].reshape(own_members, depth, cols),
            part[cut : cut + depth - 1],
            part[cut + depth - 1 : cut + 2 * (depth - 1)],
            part[cut + 2 * (depth - 1) :].reshape(2, -1, cols),
        )
        for part in (before, after)
    ]
    field_now = jnp.concatenate([pieces[0][0], current, pieces[1][0]], axis=1)
    diffusion = jnp.concatenate([pieces[0][1], diffusivity, pieces[1][1]], axis=0)
    wide_mask = jnp.concatenate([pieces[0][2], sea_mask, pieces[1][2]], axis=0)
    for substep in range(depth):
        span = slice(substep, diffusion.shape[0] - substep)
        field_now = relax(field_now, diffusion[span], wide_mask[span])
    newest = field_now.astype(jnp.bfloat16)
    obs_count = obs_cell.shape[0]
    own_info = jnp.stack([obs_value, obs_weight]).reshape(2, -1, cols)
    window_info = jnp.concatenate([pieces[0][3], own_info, pieces[1][3]], axis=1)
    group_size = lax.axis_size(("lag", "member"))
    group_rank = lax.axis_index(("lag", "member"))
    by_row = newest.transpose(1, 0, 2)
    everyone = group_gather(by_row, 1)
    members = group_size * own_members
    vmem, smem = pltpu.VMEM, pltpu.SMEM
    my_cell = lax.dynamic_slice_in_dim(
        obs_cell, lax.axis_index("member") * (obs_count // 2), obs_count // 2, 0
    )
    sampled = vmem_call(
        sample_kernel,
        jax.ShapeDtypeStruct((members, obs_count // 2), jnp.bfloat16),
        [pltpu.VMEM((rows * cols, LANES), jnp.float32), pltpu.VMEM((LANES, LANES), jnp.float32)],
        (smem, vmem),
        10**8,
    )(my_cell, everyone)
    window = sample_halo(sampled, 2)
    share = tile_obs.shape[0] // group_size
    first_tile = group_rank * share
    my_index = lax.dynamic_slice_in_dim(tile_obs, first_tile, share, 0).reshape(-1)
    my_count = lax.dynamic_slice_in_dim(tile_count, first_tile, share, 0)
    mine = vmem_call(
        mixing_kernel,
        jax.ShapeDtypeStruct((share, members // 2, 2 * members), jnp.bfloat16),
        [
            pltpu.VMEM((3 * obs_count, LANES), jnp.float32),
            pltpu.VMEM((tile_obs.shape[1], LANES), jnp.float32),
            pltpu.VMEM((share, LANES, LANES), jnp.float32),
            pltpu.VMEM((members, members, share), jnp.float32),
            pltpu.VMEM((members, members, share), jnp.float32),
            pltpu.VMEM((share, members, members), jnp.float32),
        ],
        (smem, smem, vmem, vmem),
        10**9,
    )(my_count, my_index, window, window_info)
    mixing = group_gather(mine, 3)
    mixing = mixing.reshape(-1, members // 2, 2 * members)
    member_rank = lax.axis_index("member")
    half_members = snapshots.shape[1]
    snap_mix = lax.dynamic_slice_in_dim(mixing, member_rank * members, members, 2)
    first_member = group_rank * own_members
    field_mix = lax.dynamic_slice(
        mixing,
        (0, first_member % half_members, first_member // half_members * members),
        (mixing.shape[0], own_members, members),
    )
    snaps = lax.all_gather(snapshots[0].transpose(1, 0, 2), "member", axis=0)
    smoothed, analysis = vmem_call(
        update_kernel,
        (
            jax.ShapeDtypeStruct((rows, half_members, cols), jnp.bfloat16),
            jax.ShapeDtypeStruct((rows, own_members, cols), jnp.bfloat16),
        ),
        [],
        (vmem,) * 4,
        10**8,
    )(snaps, snap_mix, everyone, field_mix)
    return (smoothed.transpose(1, 0, 2)[None], analysis.transpose(1, 0, 2))


def solution(mesh):
    placed = (
        P(("groups", "lag"), "member", "region", None),
        P(("groups", "lag", "member"), "region", None),
        P("region", None),
        P("region", None),
        P(("groups", "region")),
        P(("groups", "region")),
        P(("groups", "region")),
        P(("groups", "region"), None),
        P(("groups", "region")),
    )
    return jax.shard_map(
        local,
        mesh=mesh,
        in_specs=placed,
        out_specs=(
            P(("groups", "lag"), "member", "region", None),
            P(("groups", "lag", "member"), "region", None),
        ),
        check_vma=False,
    )
```
